512 devices in a mesh: role: 2 (over core), ep: 128 (over z, x_lo, y), tp: 2 (over x_hi).
Axes of the slice: x: 4 (x_hi: 2, x_lo: 2; x = x_hi * 2 + x_lo), y: 8, z: 8, core: 2. Of those that a mesh axis runs over, the one named last changes fastest.
Arguments:
- pool_rows: bfloat16 [2, 1024, 7168], P('role', 'ep'), may hold values from -6 to 6
- kv_weight: bfloat16 [7168, 576], P('ep', ('role', 'tp')), may hold values from -0.0625 to 0.0625
- kv_gain: float32 [512], replicated, may hold values from 0.5 to 1.5
- latent_cache: bfloat16 [1024, 48, 576], P('ep'), may hold values from -4 to 4
- queries: bfloat16 [1024, 128, 576], P('ep', ('role', 'tp')), may hold values from -28 to 28
- cache_lengths: int32 [1024], P('ep'), may hold values from 2 to 48
- partner: int32 [128], replicated, may hold values from 0 to 127, each once
- expert_ids: int32 [1024, 8], P('ep'), may hold values from 0 to 15, all different within a row; in each aligned block of 8 rows (0 to 7, 8 to 15, ...) at most 8 rows name the same one
- expert_weights: float32 [1024, 8], P('ep'), may hold values from 0.05 to 0.5
- moe_gain: float32 [7168], replicated, may hold values from 0.5 to 1.5
- gate_up: bfloat16 [128, 7168, 512], P('ep', ('role', 'tp')), may hold values from -0.0625 to 0.0625
- down_proj: bfloat16 [128, 256, 7168], P('ep', None, ('role', 'tp')), may hold values from -0.125 to 0.125
Outputs:
- attention_out: bfloat16 [1024, 128, 512], P('ep', ('role', 'tp'))
- moe_out: bfloat16 [1024, 7168], P('ep', ('role', 'tp'))
The draws below stay inside these ranges and needn't reach their ends.
Inputs may be any that keep to these rules, and one draw needn't show every extreme that they name: `expert_ids`: in each aligned block of 8 rows (the rows of one decode index) no expert is named by more than 8 rows; each row names 8 different experts. `partner`: A permutation of the decode indices.
All inputs are finite; a program needn't handle non-finite values.
Results may differ from the reference program's by a relative error of at most 0.0075.
Values may be sent and summed in bfloat16 or wider, within the bound.
A program may use at most 64 MiB of HBM per device.

```python
import math
import jax
import jax.numpy as jnp
import numpy as np
from jax import lax

D = 7168
LATENT = 512
ROPE = 64
NOPE = 128
HEADS = 128
TOPK = 8
EXPERT_FF = 2048
KV = 576
EXPERTS = 16
SPLIT = 8
FFD = 256
ROWS = 8
CACHE = 48
CAP = 8
N_ROLE = 2
N_EP = 128


def cache_base(key):
    return jnp.clip(jax.random.normal(key, (N_EP * ROWS, CACHE, KV), jnp.float32), -4.0, 4.0)


def draw_latent_cache(key, part):
    base_values = cache_base(key)
    return base_values.astype(jnp.bfloat16)


def draw_queries(key, part):
    key = jax.random.fold_in(key, 12)
    first_key = jax.random.fold_in(key, 0)
    values = jnp.clip(jax.random.normal(first_key, (N_EP * ROWS, HEADS, KV), jnp.float32), -4.0, 4.0)
    return values.astype(jnp.bfloat16)


def draw_cache_lengths(key, part):
    key = jax.random.fold_in(key, 13)
    first_key, second_key = jax.random.split(key)
    lengths = jax.random.randint(first_key, (N_EP * ROWS,), 2, CACHE + 1)
    chosen_spot = jax.random.randint(second_key, (), 0, N_EP * ROWS)
    return jnp.where(jnp.arange(N_EP * ROWS) == chosen_spot, CACHE, lengths).astype(jnp.int32)


def shard_levels(key, extent, shards, low, top_value):
    def one(dim, parts):
        heights = jax.random.uniform(jax.random.fold_in(jax.random.fold_in(key, 6), dim), (parts,), jnp.float32, low / len(shards), top_value / len(shards))
        return jnp.repeat(jnp.exp(heights), extent[dim] // parts).reshape((-1,) + (1,) * (len(extent) - dim - 1))

    level = one(*shards[0])
    for cut in shards[1:]:
        level = level * one(*cut)
    return level


def assign_block(own_key, own, number, rows, count, top, most, slope):
    ranking = jax.random.permutation(own_key, count)
    packed, ordinary = load_shares(count, rows * top, most, slope, True), load_shares(count, rows * top, most, slope, False)
    places = jnp.arange(count)

    def named(tallies, offset_by):
        used = int((tallies > 0).sum())
        fixed = max(1, used // 4)
        passed = fixed + (places - fixed + offset_by * (used - fixed)) % max(1, count - fixed)
        return jnp.zeros((count,), jnp.int32).at[ranking[jnp.where(places < fixed, places, passed)]].set(jnp.asarray(tallies, jnp.int32))

    tallies = jnp.where(number % 4 == 0, named(packed, number // 4), named(ordinary, number - number // 4 - 1))
    mixed = jax.random.permutation(jax.random.fold_in(own, 3), count)
    giver, sink = mixed[0:count // 2 * 2:2], mixed[1:count // 2 * 2:2]
    margin = jnp.minimum(tallies[giver] - 1, most - tallies[sink]) // 2
    margin = jnp.where((giver == ranking[0]) | (sink == ranking[0]) | (tallies[sink] == 0), 0, jnp.maximum(margin, 0))
    passed = jax.random.randint(jax.random.fold_in(own, 4), (count // 2,), 0, 1 << 20) % (margin + 1)
    tallies = tallies.at[giver].add(-passed).at[sink].add(passed)
    members = jnp.searchsorted(jnp.cumsum(tallies), jnp.arange(rows * top), side="right").astype(jnp.int32)
    listing = members.reshape(top, rows).T
    listing = listing[jax.random.permutation(jax.random.fold_in(own, 1), rows)]
    offset_by = jax.random.randint(jax.random.fold_in(own, 2), (rows, 1), 0, top)
    return jnp.take_along_axis(listing, (jnp.arange(top)[None, :] + offset_by) % top, axis=1)


def load_shares(count, total, bound, slope, full):
    loads = [(1 << 20) // math.isqrt(rank ** slope) + 1 for rank in range(1, count + 1)]
    largest = bound if full else min(bound, max(-(-total // count), total * loads[0] // sum(loads)))
    least = 1 if total - largest >= count - 1 else 0
    holding, rest = [largest] + [least] * (count - 1), total - largest - least * (count - 1)
    while rest > 0:
        candidates = [i for i in range(1, count) if holding[i] < largest] or [i for i in range(1, count) if holding[i] < bound]
        mass, budget = sum([loads[i] for i in candidates]), rest
        for i in candidates:
            more = min(bound - holding[i], max(1, budget * loads[i] // mass), rest)
            holding[i] = holding[i] + more
            rest = rest - more
    return np.array(holding)


def centred(rng, dims, spread, limit, cuts=(), kind=jnp.bfloat16):
    loudness = shard_levels(rng, dims, cuts, -0.22, 0.18) if cuts else 1.0
    values = jax.random.normal(rng, dims, jnp.float32) * spread * loudness
    return jnp.minimum(jnp.maximum(values, -limit), limit).astype(kind)


def setup_inputs(seed: int = 0) -> dict:
    key_of = jax.random.split(jax.random.key(seed), 13)
    pool_rows = centred(key_of[0], (N_ROLE, N_EP * ROWS, D), 1.0, 6.0, ((0, 2), (1, 128)))
    kv_weight = centred(key_of[1], (D, KV), D ** -0.5, 0.0625, ((0, 128), (1, 4)))
    kv_gain = jnp.clip(1.0 + 0.1 * jax.random.normal(key_of[2], (LATENT,), jnp.float32), 0.5, 1.5)
    latent_cache = draw_latent_cache(jax.random.fold_in(key_of[12], 71), 0)
    queries = draw_queries(jax.random.fold_in(key_of[12], 71), 0)
    cache_lengths = draw_cache_lengths(jax.random.fold_in(key_of[12], 71), 0)
    partner = jax.random.permutation(key_of[6], N_EP).astype(jnp.int32)
    expert_ids_keys = jax.random.split(jax.random.fold_in(key_of[7], 1), (N_EP * ROWS) // ROWS)
    expert_ids_turns = jax.random.permutation(jax.random.fold_in(key_of[7], 3), (N_EP * ROWS) // ROWS)
    expert_ids = jax.vmap(lambda own, number: assign_block(jax.random.fold_in(key_of[7], 2), own, number, ROWS, EXPERTS, TOPK, CAP, 2))(expert_ids_keys, expert_ids_turns).reshape((N_EP * ROWS, TOPK))
    expert_weights = jnp.clip(0.05 + 0.45 * jax.random.uniform(key_of[8], (N_EP * ROWS, TOPK), jnp.float32) ** shard_levels(key_of[8], (N_EP * ROWS, TOPK), ((0, 128),), -0.2, 0.2), 0.05, 0.5)
    moe_gain = jnp.clip(1.0 + 0.1 * jax.random.normal(key_of[9], (D,), jnp.float32), 0.5, 1.5)
    gate_up = centred(key_of[10], (EXPERTS * SPLIT, D, 2 * FFD), D ** -0.5, 0.0625, ((0, 128), (1, 4)))
    down_proj = centred(key_of[11], (EXPERTS * SPLIT, FFD, D), EXPERT_FF ** -0.5, 0.125, ((0, 128), (2, 4)))
    return dict(pool_rows=pool_rows, kv_weight=kv_weight, kv_gain=kv_gain, latent_cache=latent_cache, queries=queries, cache_lengths=cache_lengths, partner=partner, expert_ids=expert_ids, expert_weights=expert_weights, moe_gain=moe_gain, gate_up=gate_up, down_proj=down_proj)


EPSILON = 1e-06

def make_keys(raw_rows, positions, kv_gain):
    as_float = raw_rows.astype(jnp.float32)
    latent_part = as_float[:, :LATENT]
    inverse_rms = lax.rsqrt(lax.optimization_barrier(jnp.mean(latent_part * latent_part, axis=1, keepdims=True)) + EPSILON)
    latent_part = latent_part * inverse_rms * kv_gain.astype(jnp.float32)[None, :]
    rotary_part = as_float[:, LATENT:].reshape(-1, ROPE // 2, 2)
    frequency = 10000.0 ** (-2.0 * jnp.arange(ROPE // 2, dtype=jnp.float32) / ROPE)
    angle_table = positions.astype(jnp.float32)[:, None] * frequency[None, :]
    cosine = jnp.cos(angle_table)
    sine_table = jnp.sin(angle_table)
    even_part = rotary_part[:, :, 0]
    odd_part = rotary_part[:, :, 1]
    rotated = jnp.stack([even_part * cosine - odd_part * sine_table, even_part * sine_table + odd_part * cosine], axis=2)
    return jnp.concatenate([latent_part, rotated.reshape(-1, ROPE)], axis=1).astype(jnp.bfloat16)

def attend(query_rows, cache_rows, length, prompt_key, new_key):
    score_scale = (NOPE + ROPE) ** (-0.5)
    query_float = query_rows.astype(jnp.float32)
    cache_float = cache_rows.astype(jnp.float32)
    prompt_float = prompt_key.astype(jnp.float32)
    new_float = new_key.astype(jnp.float32)
    row_count = query_rows.shape[0]
    cache_scores = jnp.einsum('rhk,rlk->rhl', query_float, cache_float) * score_scale
    valid_mask = jnp.arange(cache_rows.shape[1], dtype=jnp.int32)[None, :] < length[:, None]
    cache_scores = jnp.where(valid_mask[:, None, :], cache_scores, -jnp.inf)
    prompt_scores = jnp.einsum('rhk,ck->rhc', query_float, prompt_float) * score_scale
    leading = jnp.arange(row_count, dtype=jnp.int32) == 0
    prompt_scores = jnp.where(leading[:, None, None], prompt_scores, -jnp.inf)
    own_scores = jnp.einsum('rhk,rk->rh', query_float, new_float) * score_scale
    row_top = jnp.maximum(jnp.maximum(lax.optimization_barrier(jnp.max(cache_scores, axis=2)), lax.optimization_barrier(jnp.max(prompt_scores, axis=2))), own_scores)
    cache_exp = jnp.exp(cache_scores - row_top[:, :, None])
    prompt_exp = jnp.exp(prompt_scores - row_top[:, :, None])
    own_exp = jnp.exp(own_scores - row_top)
    denominator = lax.optimization_barrier(jnp.sum(cache_exp, axis=2)) + lax.optimization_barrier(jnp.sum(prompt_exp, axis=2)) + own_exp
    cache_weight = (cache_exp / denominator[:, :, None]).astype(jnp.bfloat16)
    prompt_weight = (prompt_exp / denominator[:, :, None]).astype(jnp.bfloat16)
    own_weight = (own_exp / denominator).astype(jnp.bfloat16)
    result = jnp.einsum('rhl,rld->rhd', cache_weight.astype(jnp.float32), cache_float[:, :, :LATENT])
    result = result + jnp.einsum('rhc,cd->rhd', prompt_weight.astype(jnp.float32), prompt_float[:, :LATENT])
    result = result + own_weight.astype(jnp.float32)[:, :, None] * new_float[:, None, :LATENT]
    return result.astype(jnp.bfloat16)

def reference(pool_rows, kv_weight, kv_gain, latent_cache, queries, cache_lengths, partner, expert_ids, expert_weights, moe_gain, gate_up, down_proj):
    total_rows = N_EP * ROWS
    raw_latent = jnp.dot(pool_rows.reshape(-1, D), kv_weight, preferred_element_type=jnp.float32)
    raw_latent = raw_latent.astype(jnp.bfloat16).reshape(N_ROLE, total_rows, KV)
    ep_names = jnp.arange(N_EP, dtype=jnp.int32)
    source_of = lax.optimization_barrier(jnp.sum(jnp.where(partner[None, :] == ep_names[:, None], ep_names[None, :], 0), axis=1)).astype(jnp.int32)
    prompt_raw = raw_latent[0].reshape(N_EP, ROWS, KV)[source_of]
    lengths_grid = cache_lengths.reshape(N_EP, ROWS)
    prompt_position = lengths_grid[:, 0][:, None] + jnp.arange(ROWS, dtype=jnp.int32)[None, :]
    prompt_keys = make_keys(prompt_raw.reshape(-1, KV), prompt_position.reshape(-1), kv_gain).reshape(N_EP, ROWS, KV)
    leading = (jnp.arange(ROWS, dtype=jnp.int32) == 0).astype(jnp.int32)
    new_position = (lengths_grid + ROWS * leading[None, :]).reshape(-1)
    new_keys = make_keys(raw_latent[1], new_position, kv_gain).reshape(N_EP, ROWS, KV)

    def attend_block(inputs):
        query_block, cache_block, length_block, prompt_block, new_block = inputs
        return attend(query_block, cache_block, length_block, prompt_block, new_block)
    attention_out = lax.map(attend_block, (queries.reshape(N_EP, ROWS, HEADS, KV), latent_cache.reshape(N_EP, ROWS, CACHE, KV), lengths_grid, prompt_keys, new_keys))
    attention_out = attention_out.reshape(total_rows, HEADS, LATENT)
    tokens = pool_rows[1].astype(jnp.float32)
    moe_input = (tokens * lax.rsqrt(lax.optimization_barrier(jnp.mean(tokens * tokens, axis=1, keepdims=True)) + EPSILON) * moe_gain[None, :]).astype(jnp.bfloat16)
    expert_names = jnp.arange(EXPERTS, dtype=jnp.int32)
    matches = expert_ids[:, :, None] == expert_names[None, None, :]
    combine_weight = lax.optimization_barrier(jnp.sum(jnp.where(matches, expert_weights[:, :, None], 0.0), axis=1)).astype(jnp.bfloat16)
    routed = jnp.any(matches, axis=1)
    shard_routed = jnp.repeat(routed.T, SPLIT, axis=0)
    shard_weight = jnp.repeat(combine_weight.T, SPLIT, axis=0)
    most_rows = N_EP * CAP

    def expert_step(running, inputs):
        up_table, down_table, routed_column, weight_column = inputs
        order = jnp.argsort(jnp.where(routed_column, 0, 1).astype(jnp.int32), stable=True)[:most_rows].astype(jnp.int32)
        chosen = moe_input[order]
        chosen_weight = jnp.where(routed_column[order], weight_column[order].astype(jnp.float32), 0.0)
        projected = jnp.dot(chosen, up_table, preferred_element_type=jnp.float32)
        hidden_units = (jax.nn.silu(projected[:, :FFD]) * projected[:, FFD:]).astype(jnp.bfloat16)
        partial_out = jnp.dot(hidden_units, down_table, preferred_element_type=jnp.float32).astype(jnp.bfloat16)
        return (running.at[order].add(chosen_weight[:, None] * partial_out.astype(jnp.float32)), None)
    moe_sum, unused = lax.scan(expert_step, jnp.zeros((total_rows, D), jnp.float32), (gate_up, down_proj, shard_routed, shard_weight))
    return (attention_out, moe_sum.astype(jnp.bfloat16))
```

```python
import functools

import jax
import jax.numpy as jnp
from jax import lax
from jax.experimental import pallas as pl
from jax.experimental.pallas import tpu as pltpu
from jax.sharding import PartitionSpec as P

MESH = pl.DeviceIdType.MESH
BF = jnp.bfloat16
F32 = jnp.float32
LATENT = 512
ROPE = 64
NOPE = 128
NX = 2
EPSILON = 1e-06


def make_keys(raw_rows, positions, kv_gain):
    as_float = raw_rows.astype(jnp.float32)
    latent_part = as_float[:, :LATENT]
    inverse_rms = lax.rsqrt(jnp.mean(latent_part * latent_part, axis=1, keepdims=True) + EPSILON)
    latent_part = latent_part * inverse_rms * kv_gain[None, :]
    rotary_part = as_float[:, LATENT:].reshape(-1, ROPE // 2, 2)
    frequency = 10000.0 ** (-2.0 * jnp.arange(ROPE // 2, dtype=jnp.float32) / ROPE)
    angle_table = positions.astype(jnp.float32)[:, None] * frequency[None, :]
    cosine = jnp.cos(angle_table)
    sine_table = jnp.sin(angle_table)
    even_part = rotary_part[:, :, 0]
    odd_part = rotary_part[:, :, 1]
    rotated = jnp.stack(
        [even_part * cosine - odd_part * sine_table, even_part * sine_table + odd_part * cosine],
        axis=2,
    )
    return jnp.concatenate([latent_part, rotated.reshape(-1, ROPE)], axis=1).astype(jnp.bfloat16)


def attend(query_rows, cache_rows, length, prompt_key, new_key):
    score_scale = (NOPE + ROPE) ** (-0.5)
    row_count = query_rows.shape[0]
    cache_scores = (
        jnp.einsum("rhk,rlk->rhl", query_rows, cache_rows, preferred_element_type=jnp.float32)
        * score_scale
    )
    valid_mask = jnp.arange(cache_rows.shape[1], dtype=jnp.int32)[None, :] < length[:, None]
    cache_scores = jnp.where(valid_mask[:, None, :], cache_scores, -jnp.inf)
    prompt_scores = (
        jnp.einsum("rhk,ck->rhc", query_rows, prompt_key, preferred_element_type=jnp.float32)
        * score_scale
    )
    leading = jnp.arange(row_count, dtype=jnp.int32) == 0
    prompt_scores = jnp.where(leading[:, None, None], prompt_scores, -jnp.inf)
    own_scores = (
        jnp.einsum("rhk,rk->rh", query_rows, new_key, preferred_element_type=jnp.float32)
        * score_scale
    )
    row_top = jnp.maximum(
        jnp.maximum(jnp.max(cache_scores, axis=2), jnp.max(prompt_scores, axis=2)), own_scores
    )
    cache_exp = jnp.exp(cache_scores - row_top[:, :, None])
    prompt_exp = jnp.exp(prompt_scores - row_top[:, :, None])
    own_exp = jnp.exp(own_scores - row_top)
    denominator = jnp.sum(cache_exp, axis=2) + jnp.sum(prompt_exp, axis=2) + own_exp
    cache_weight = (cache_exp / denominator[:, :, None]).astype(jnp.bfloat16)
    prompt_weight = (prompt_exp / denominator[:, :, None]).astype(jnp.bfloat16)
    own_weight = (own_exp / denominator).astype(jnp.bfloat16)
    result = jnp.einsum(
        "rhl,rld->rhd", cache_weight, cache_rows[:, :, :LATENT], preferred_element_type=jnp.float32
    )
    result = result + jnp.einsum(
        "rhc,cd->rhd", prompt_weight, prompt_key[:, :LATENT], preferred_element_type=jnp.float32
    )
    result = result + own_weight.astype(jnp.float32)[:, :, None] * new_key[:, None, :LATENT].astype(
        jnp.float32
    )
    return result.astype(jnp.bfloat16)


def fused_kernel(
    n, tok, gain, ids, wts, gu, dn, kvw, sel, asrc,
    moe_out, new_out, prompt_out,
    xsend, xpair, xg, pf, ps, pr, hb, out, cr, fs, cf,
    ts, tr, wb, pk, pkr, rn, ry, rzs, rz, rp,
    a0r, a1r, a2r, b1r, b2r, c2r, k5n, k7r, one, snd,
):
    role, ep, tp = lax.axis_index("role"), lax.axis_index("ep"), lax.axis_index("tp")
    z, x, y = ep // (NX * n), (ep // n) % NX, ep % n
    a_me = ep // n
    na = NX * n
    half = n // 2
    ch = n // 2
    ds = gu.shape[0]
    fe, kc = kvw.shape
    fa = n * fe
    group = role * 2 + tp

    def dev(r, zz, xx, yy, t):
        return (r, (zz * NX + xx) * n + yy, t)

    def slot(s, h, d):
        if s == 0:
            return h
        if s == half:
            return 2 + (half - 1) * 4 + h
        return 2 + (s - 1) * 4 + 2 * h + d

    n_sets = 2 + (half - 1) * 4 + 2

    def rcopy(src, dst, s, r, device):
        return pltpu.make_async_remote_copy(
            src_ref=src, dst_ref=dst, send_sem=s, recv_sem=r, device_id=device, device_id_type=MESH
        )

    def drain(ref, sem):
        pltpu.make_async_copy(ref, ref, sem).wait()

    barrier = pltpu.get_barrier_semaphore()
    others = 0
    for xx in (0, 1):
        ox = (x + xx) % NX
        for d in range(n):
            if xx == 0 and d == 0:
                continue
            pl.semaphore_signal(
                barrier, inc=1, device_id=dev(role, z, ox, (y + d) % n, tp), device_id_type=MESH
            )
            others += 1
            if d:
                pl.semaphore_signal(
                    barrier, inc=1, device_id=dev(role, (z + d) % n, ox, y, tp), device_id_type=MESH
                )
                others += 1
    peers = [((role + (k >> 1)) % 2, (tp + (k & 1)) % 2) for k in range(4)]
    for k in (1, 2, 3):
        pl.semaphore_signal(
            barrier, inc=1, device_id=dev(peers[k][0], z, x, y, peers[k][1]), device_id_type=MESH
        )
        others += 1
    pl.semaphore_signal(
        barrier, inc=1, device_id=dev(1 - role, z, 1 - x, y, tp), device_id_type=MESH
    )
    others += 1
    pl.semaphore_wait(barrier, others)

    @pl.when(role == 1)
    def _():
        xf = tok[...].astype(F32)
        inv = lax.rsqrt(jnp.mean(xf * xf, axis=1, keepdims=True) + EPSILON)
        lanes = lax.broadcasted_iota(jnp.int32, (8, 128), 1)
        comb = jnp.zeros((8, 128), F32)
        for k in range(ids.shape[1]):
            comb = comb + jnp.where(lanes == ids[:, k : k + 1], wts[:, k : k + 1], 0.0)
        for r in (0, 1):
            cols = pl.ds(pl.multiple_of((2 * r + tp) * ds, 128), ds)
            part = (tok[:, cols].astype(F32) * inv * gain[:, cols]).astype(BF)
            if r == 0:
                xsend[:, :ds] = part
                xsend[:, ds:] = comb.astype(BF)
            else:
                xpair[x, :, :ds] = part
                xpair[x, :, ds:] = comb.astype(BF)
        rcopy(xsend, xpair.at[x], snd.at[0], a0r.at[0], dev(0, z, x, y, tp)).start()
        rcopy(xsend, xpair.at[x], snd.at[1], a0r.at[1], dev(0, z, 1 - x, y, tp)).start()
        rcopy(xpair.at[x], xpair.at[x], snd.at[2], a0r.at[1], dev(1, z, 1 - x, y, tp)).start()

    def latent_send():
        for a in range(na):
            ts[a] = tok[:, a * fa : (a + 1) * fa]
        for d in range(1, na):
            ap = (a_me + d) % na
            rcopy(ts.at[ap], tr.at[a_me], snd.at[3], one.at[0], dev(role, ap // NX, ap % NX, y, tp)).start()
        for d in range(1, n):
            rcopy(kvw, wb.at[role, y], snd.at[4], one.at[1], dev(role, z, x, (y + d) % n, tp)).start()
        tr[a_me] = ts[a_me]
        wb[role, y] = kvw[...]

    def latent_swap():
        drain(wb.at[role, 0 : n - 1], one.at[1])
        rcopy(wb.at[role], wb.at[role], snd.at[5], one.at[2], dev(1 - role, z, x, y, tp)).start()

    def latent_project():
        drain(tr.at[0 : na - 1], one.at[0])
        drain(wb.at[0], one.at[2])
        rows = lax.broadcasted_iota(jnp.int32, (kc, 2 * kc), 0)
        cols = lax.broadcasted_iota(jnp.int32, (kc, 2 * kc), 1)
        weight = jnp.zeros((fa, 2 * kc), F32)
        for r in (0, 1):
            place = jnp.where(cols == rows + r * kc, 1.0, 0.0).astype(BF)
            block = wb[r].astype(F32).reshape(fa, kc).astype(BF)
            weight = weight + jnp.dot(block, place, preferred_element_type=F32)
        tokens = tr[...].astype(F32).reshape(na * 8, fa).astype(BF)
        share = jnp.dot(tokens, weight.astype(BF), preferred_element_type=F32)
        pk[...] = share.reshape(na, 8, 2 * kc)
        for d in range(1, na):
            ap = (a_me + d) % na
            rcopy(pk.at[ap], pkr.at[a_me], snd.at[6], one.at[3], dev(role, ap // NX, ap % NX, y, tp)).start()
        pkr[a_me] = pk[a_me]

    def latent_sum():
        drain(pkr.at[0 : na - 1], one.at[3])
        raw = jnp.sum(pkr[...], axis=0).astype(BF)

        @pl.when(role == 1)
        def _():
            rn[tp] = raw
            for k in (1, 2, 3):
                rcopy(
                    rn.at[tp], rn.at[tp], snd.at[7], k5n.at[tp], dev(peers[k][0], z, x, y, peers[k][1])
                ).start()

        @pl.when(role == 0)
        def _():
            ry[y] = raw
            for d in range(1, n):
                rcopy(ry.at[y], ry.at[y], snd.at[8], one.at[4], dev(role, z, x, (y + d) % n, tp)).start()

    def handoff_send():
        @pl.when(role == 0)
        def _():
            drain(ry.at[0 : n - 1], one.at[4])
            for a in range(na):
                rzs[a] = ry[sel[0, a]]
            for d in range(1, na):
                ap = (a_me + d) % na
                rcopy(rzs.at[ap], rz.at[a_me], snd.at[9], one.at[5], dev(role, ap // NX, ap % NX, y, tp)).start()
            rz[a_me] = rzs[a_me]

    def handoff_share():
        @pl.when(role == 0)
        def _():
            drain(rz.at[0 : na - 1], one.at[5])
            rp[tp] = rz[asrc[0, 0]]
            for k in (1, 2, 3):
                rcopy(
                    rp.at[tp], rp.at[tp], snd.at[10], k7r.at[tp], dev(peers[k][0], z, x, y, peers[k][1])
                ).start()

    def raw_rows():
        for t in (0, 1):
            @pl.when(jnp.logical_not(jnp.logical_and(role == 1, tp == t)))
            def _():
                drain(rn.at[t], k5n.at[t])

            @pl.when(jnp.logical_not(jnp.logical_and(role == 0, tp == t)))
            def _():
                drain(rp.at[t], k7r.at[t])

        rows = lax.broadcasted_iota(jnp.int32, (2 * kc, 4 * kc), 0)
        cols = lax.broadcasted_iota(jnp.int32, (2 * kc, 4 * kc), 1)
        new = jnp.zeros((8, 4 * kc), F32)
        prompt = jnp.zeros((8, 4 * kc), F32)
        for t in (0, 1):
            target = rows + t * kc + jnp.where(rows >= kc, kc, 0)
            place = jnp.where(cols == target, 1.0, 0.0).astype(BF)
            new = new + jnp.dot(rn[t], place, preferred_element_type=F32)
            prompt = prompt + jnp.dot(rp[t], place, preferred_element_type=F32)
        new_out[...] = new
        prompt_out[...] = prompt

    h_me = (y + z) % 2
    j_me = jnp.where(h_me == 0, y // 2, z // 2)

    def neighbour(h, step):
        if h == 0:
            return dev(role, (z + step) % n, x, y, tp)
        return dev(role, z, x, (y + step) % n, tp)

    def gather_start():
        @pl.when(role == 0)
        def _():
            drain(xpair.at[0], a0r.at[0])

        drain(xpair.at[0], a0r.at[1])
        pair = jnp.concatenate([xpair[0].astype(F32), xpair[1].astype(F32)], axis=0)
        xg[h_me, j_me] = pair.astype(BF)
        for d in range(1, n):
            where = dev(role, (z + d * h_me) % n, x, (y + d * (1 - h_me)) % n, tp)
            rcopy(xg.at[h_me, j_me], xg.at[h_me, j_me], snd.at[11], a1r.at[h_me, j_me], where).start()

    def own_or(h, j, yes, no):
        mine = jnp.logical_and(h_me == h, j_me == j)
        pl.when(jnp.logical_not(mine))(no)
        if yes is not None:
            pl.when(mine)(yes)

    def gather_step(s):
        for j in range(ch):
            for h in (0, 1):
                for d in (0, 1):
                    reach = half - d
                    if s == 0:
                        if d == 0:
                            own_or(h, j, None, lambda: drain(xg.at[h, j], a1r.at[h, j]))
                        here = xg.at[h, j]
                    else:
                        if s > reach:
                            continue
                        here = xg.at[slot(s, h, d), j]
                        drain(here, a2r.at[slot(s, h, d), j])
                    if s + 1 <= reach:
                        nxt = slot(s + 1, h, d)
                        rcopy(
                            here, xg.at[nxt, j], snd.at[12], a2r.at[nxt, j], neighbour(h, 1 - 2 * d)
                        ).start()

    def span(s):
        lo = slot(s, 0, 0)
        hi = slot(s + 1, 0, 0) if s < half else n_sets
        return lo, hi

    def project_step(s):
        lo, hi = span(s)
        m = (hi - lo) * ch * 16
        r0 = lo * ch * 16
        q = m // 4
        rows = xg[lo:hi].reshape(m, ds + 128)
        share = jnp.dot(rows[:, :ds], gu[...], preferred_element_type=F32)
        pf[r0 : r0 + m] = share
        ps[r0 : r0 + m] = share.astype(BF)
        for k in (1, 2, 3):
            there = pl.ds(pl.multiple_of(r0 + (peers[k][0] * 2 + peers[k][1]) * q, q), q)
            rcopy(
                ps.at[there], pr.at[k - 1, r0 // 4 : r0 // 4 + q], snd.at[13], b1r.at[s, k - 1],
                dev(peers[k][0], z, x, y, peers[k][1]),
            ).start()

    def hidden_step(s):
        lo, hi = span(s)
        m = (hi - lo) * ch * 16
        r0 = lo * ch * 16
        q = m // 4
        mine = pl.ds(pl.multiple_of(r0 + group * q, q), q)
        total = pf[mine]
        for k in (1, 2, 3):
            part = pr.at[k - 1, r0 // 4 : r0 // 4 + q]
            drain(part, b1r.at[s, k - 1])
            total = total + part[...].astype(F32)
        width = total.shape[1] // 2
        gate = total[:, :width]
        hb[mine] = (gate / (1.0 + jnp.exp(-gate)) * total[:, width:]).astype(BF)
        for k in (1, 2, 3):
            rcopy(
                hb.at[mine], hb.at[mine], snd.at[14], b2r.at[s, k - 1],
                dev(peers[k][0], z, x, y, peers[k][1]),
            ).start()

    def down_step(s):
        lo, hi = span(s)
        m = (hi - lo) * ch * 16
        r0 = lo * ch * 16
        q = m // 4
        for k in (1, 2, 3):
            drain(hb.at[0:q], b2r.at[s, k - 1])
        part = jnp.dot(hb[r0 : r0 + m], dn[...], preferred_element_type=F32)
        lanes = lax.broadcasted_iota(jnp.int32, (m, 128), 1)
        table = xg[lo:hi].reshape(m, ds + 128)[:, ds:].astype(F32)
        weight = jnp.sum(jnp.where(lanes == a_me, table, 0.0), axis=1, keepdims=True)
        out[lo:hi] = (part * weight).astype(BF).reshape(hi - lo, ch, 16, ds)

    def cslot(s, h, d):
        if s == 0:
            return h if d == 0 else n_sets + h
        return slot(s, h, d)

    def sum_step(s):
        for j in range(ch):
            for h in (0, 1):
                for d in (0, 1):
                    reach = half - d
                    if s > reach:
                        continue
                    if s == reach:
                        here = out.at[slot(s, h, d), j]
                    else:
                        here = cr.at[cslot(s, h, d), j]
                        drain(here, c2r.at[cslot(s, h, d), j])
                        here[...] = (
                            here[...].astype(F32) + out[slot(s, h, d), j].astype(F32)
                        ).astype(BF)
                    to = cslot(s - 1, h, d)
                    rcopy(
                        here, cr.at[to, j], snd.at[15], c2r.at[to, j], neighbour(h, 2 * d - 1)
                    ).start()

    def deliver():
        for j in range(ch):
            for h in (0, 1):
                total = out[h, j].astype(F32)
                for d in (0, 1):
                    if half - d < 1:
                        continue
                    here = cr.at[cslot(0, h, d), j]
                    drain(here, c2r.at[cslot(0, h, d), j])
                    total = total + here[...].astype(F32)
                if h == 0:
                    zz, yy, at = z, 2 * j + z % 2, y * NX + x
                else:
                    zz, yy, at = 2 * j + (1 - y % 2), y, z * NX + x
                for xd in (0, 1):
                    piece = fs.at[h, j, xd]
                    piece[...] = total[8 * xd : 8 * xd + 8].astype(BF)
                    itself = jnp.logical_and(jnp.logical_and(h_me == h, j_me == j), x == xd)

                    @pl.when(itself)
                    def _():
                        cf[at] = piece[...]

                    @pl.when(jnp.logical_not(itself))
                    def _():
                        rcopy(
                            piece, cf.at[at], snd.at[16], one.at[6], dev(role, zz, xd, yy, tp)
                        ).start()

    latent_send()
    gather_start()
    latent_swap()
    gather_step(0)
    latent_project()
    project_step(0)
    for s in range(1, half + 1):
        gather_step(s)
        if s == 1:
            latent_sum()
        if s == 2:
            handoff_send()
        if s == 3:
            handoff_share()
        project_step(s)
        hidden_step(s - 1)
        if s >= 2:
            down_step(s - 2)
    hidden_step(half)
    down_step(half - 1)
    down_step(half)
    for s in range(half, 0, -1):
        sum_step(s)
    deliver()
    raw_rows()
    drain(cf.at[0 : 2 * n - 1], one.at[6])
    moe_out[...] = jnp.sum(cf[...].astype(F32), axis=0).astype(BF)

    @pl.when(role == 1)
    def _():
        for i in (0, 1, 2):
            drain(xsend, snd.at[i])
        drain(rz.at[0:3], snd.at[7])

    @pl.when(role == 0)
    def _():
        drain(ry.at[0 : n - 1], snd.at[8])
        drain(rz.at[0 : na - 1], snd.at[9])
        drain(rz.at[0:3], snd.at[10])

    drain(tr.at[0 : na - 1], snd.at[3])
    drain(wb.at[0, 0 : n - 1], snd.at[4])
    drain(wb.at[0], snd.at[5])
    drain(pkr.at[0 : na - 1], snd.at[6])
    drain(xg.at[0 : n - 1, 0], snd.at[11])
    drain(xg.at[0 : 2 * (n - 1)], snd.at[12])
    rows = ps.shape[0] // 4 * 3
    drain(ps.at[0:rows], snd.at[13])
    drain(hb.at[0:rows], snd.at[14])
    drain(cr.at[0 : 2 * (n - 1)], snd.at[15])
    drain(cf.at[0 : 2 * n - 1], snd.at[16])


def fused(n, tok, gain, ids, wts, gu, dn, kvw, sel, asrc):
    half = n // 2
    ch = n // 2
    n_sets = 2 + (half - 1) * 4 + 2
    total_rows = n_sets * ch * 16
    ds, f2 = gu.shape
    dsx = ds + 128
    fe, kc = kvw.shape
    na = NX * n
    vm = pl.BlockSpec(memory_space=pltpu.VMEM)
    sm = pl.BlockSpec(memory_space=pltpu.SMEM)
    dma = pltpu.SemaphoreType.DMA
    scratch = [
        pltpu.VMEM((8, dsx), BF),
        pltpu.VMEM((2, 8, dsx), BF),
        pltpu.VMEM((n_sets, ch, 16, dsx), BF),
        pltpu.VMEM((total_rows, f2), F32),
        pltpu.VMEM((total_rows, f2), BF),
        pltpu.VMEM((3, total_rows // 4, f2), BF),
        pltpu.VMEM((total_rows, f2 // 2), BF),
        pltpu.VMEM((n_sets, ch, 16, ds), BF),
        pltpu.VMEM((n_sets + 2, ch, 16, ds), BF),
        pltpu.VMEM((2, ch, 2, 8, ds), BF),
        pltpu.VMEM((2 * n, 8, ds), BF),
        pltpu.VMEM((na, 8, n * fe), BF),
        pltpu.VMEM((na, 8, n * fe), BF),
        pltpu.VMEM((2, n, fe, kc), BF),
        pltpu.VMEM((na, 8, 2 * kc), F32),
        pltpu.VMEM((na, 8, 2 * kc), F32),
        pltpu.VMEM((2, 8, 2 * kc), BF),
        pltpu.VMEM((n, 8, 2 * kc), BF),
        pltpu.VMEM((na, 8, 2 * kc), BF),
        pltpu.VMEM((na, 8, 2 * kc), BF),
        pltpu.VMEM((2, 8, 2 * kc), BF),
        dma((2,)),
        dma((2, ch)),
        dma((n_sets, ch)),
        dma((half + 1, 3)),
        dma((half + 1, 3)),
        dma((n_sets + 2, ch)),
        dma((2,)),
        dma((2,)),
        dma((7,)),
        dma((17,)),
    ]
    return pl.pallas_call(
        functools.partial(fused_kernel, n),
        out_shape=(
            jax.ShapeDtypeStruct((8, ds), BF),
            jax.ShapeDtypeStruct((8, 4 * kc), F32),
            jax.ShapeDtypeStruct((8, 4 * kc), F32),
        ),
        in_specs=[vm] * 7 + [sm] * 2,
        out_specs=(vm, vm, vm),
        scratch_shapes=scratch,
        compiler_params=pltpu.CompilerParams(
            collective_id=0, has_side_effects=True, vmem_limit_bytes=56 * 1024 * 1024
        ),
    )(tok, gain, ids, wts, gu, dn, kvw, sel, asrc)


def per_device(
    n,
    pool_rows,
    kv_weight,
    kv_gain,
    latent_cache,
    queries,
    cache_lengths,
    partner,
    expert_ids,
    expert_weights,
    moe_gain,
    gate_up,
    down_proj,
):
    row_count = latent_cache.shape[0]
    ep = lax.axis_index("ep")
    names = jnp.arange(partner.shape[0], dtype=jnp.int32)
    wanted = jnp.arange(NX * n, dtype=jnp.int32) * n + ep % n
    source = jnp.sum(jnp.where(partner[None, :] == wanted[:, None], names[None, :], 0), axis=1)
    here = jnp.sum(jnp.where(partner == ep, names, 0))
    moe_out, new_raw, prompt_raw = fused(
        n,
        pool_rows[0],
        moe_gain[None, :],
        expert_ids,
        expert_weights,
        gate_up[0],
        down_proj[0],
        kv_weight,
        (source % n)[None, :],
        (here // n)[None, None],
    )
    leading = (jnp.arange(row_count, dtype=jnp.int32) == 0).astype(jnp.int32)
    new_keys = make_keys(new_raw, cache_lengths + row_count * leading, kv_gain)
    prompt_keys = make_keys(
        prompt_raw, cache_lengths[0] + jnp.arange(row_count, dtype=jnp.int32), kv_gain
    )
    attention_out = attend(queries, latent_cache, cache_lengths, prompt_keys, new_keys)
    return (attention_out, moe_out)


def solution(mesh):
    n = round((mesh.shape["ep"] // NX) ** 0.5)
    in_specs = (
        P("role", "ep", None),
        P("ep", ("role", "tp")),
        P(),
        P("ep", None, None),
        P("ep", ("role", "tp"), None),
        P("ep"),
        P(),
        P("ep", None),
        P("ep", None),
        P(),
        P("ep", ("role", "tp"), None),
        P("ep", None, ("role", "tp")),
    )
    out_specs = (P("ep", ("role", "tp"), None), P("ep", ("role", "tp")))
    return jax.shard_map(
        functools.partial(per_device, n),
        mesh=mesh, in_specs=in_specs, out_specs=out_specs, check_vma=False,
    )
```

```python
import functools
import math

import jax
import jax.numpy as jnp
from jax import lax
from jax.experimental import pallas as pl
from jax.experimental.pallas import tpu as pltpu
from jax.sharding import PartitionSpec as P

MESH = pl.DeviceIdType.MESH
BF = jnp.bfloat16
F32 = jnp.float32
LATENT = 512
ROPE = 64
NOPE = 128
NX = 2
EPSILON = 1e-06


def fused_kernel(
    n, tok, gain, ids, wts, part, kvg, lens, kvw, gu_hbm, dn_hbm, q_hbm, cache_hbm,
    att, moe_out,
    gu, dn, qv, kb,
    xsend, xpair, xg, pf, ps, pr, hb, out, cr, fs, cf,
    ts, tr, wb, pk, pkr, rn, ry, rzs, rz, rp, kx,
    a0r, a1r, a2r, b1r, b2r, c2r, k5n, k7r, one, snd, loc,
):
    role, ep, tp = lax.axis_index("role"), lax.axis_index("ep"), lax.axis_index("tp")
    z, x, y = ep // (NX * n), (ep // n) % NX, ep % n
    a_me = ep // n
    na = NX * n
    ch = n // 2
    cd = ch // 2
    ds = gu.shape[0]
    fe, kc = kvw.shape
    fa = n * fe
    group = role * 2 + tp

    def dev(r, zz, xx, yy, t):
        return (r, (zz * NX + xx) * n + yy, t)

    def rcopy(src, dst, s, r, device):
        return pltpu.make_async_remote_copy(
            src_ref=src, dst_ref=dst, send_sem=s, recv_sem=r, device_id=device, device_id_type=MESH
        )

    def drain(ref, sem):
        pltpu.make_async_copy(ref, ref, sem).wait()

    barrier = pltpu.get_barrier_semaphore()
    others = 0
    for xx in (0, 1):
        ox = (x + xx) % NX
        for d in range(n):
            if xx == 0 and d == 0:
                continue
            pl.semaphore_signal(
                barrier, inc=1, device_id=dev(role, z, ox, (y + d) % n, tp), device_id_type=MESH
            )
            others += 1
            if d:
                pl.semaphore_signal(
                    barrier, inc=1, device_id=dev(role, (z + d) % n, ox, y, tp), device_id_type=MESH
                )
                others += 1
    peers = [((role + (k >> 1)) % 2, (tp + (k & 1)) % 2) for k in range(4)]
    for k in (1, 2, 3):
        pl.semaphore_signal(
            barrier, inc=1, device_id=dev(peers[k][0], z, x, y, peers[k][1]), device_id_type=MESH
        )
        others += 1
    pl.semaphore_signal(
        barrier, inc=1, device_id=dev(1 - role, z, 1 - x, y, tp), device_id_type=MESH
    )
    others += 1

    load_gu = pltpu.make_async_copy(gu_hbm.at[0], gu, loc.at[0])
    load_dn = pltpu.make_async_copy(dn_hbm.at[0], dn, loc.at[1])
    load_q = pltpu.make_async_copy(q_hbm, qv, loc.at[2])
    load_cache = pltpu.make_async_copy(cache_hbm, kb.at[:, 0 : cache_hbm.shape[1]], loc.at[3])
    load_gu.start()
    load_dn.start()
    load_q.start()
    load_cache.start()

    @pl.when(role == 1)
    def _():
        xf = tok[0].astype(F32)
        inv = lax.rsqrt(jnp.mean(xf * xf, axis=1, keepdims=True) + EPSILON)
        lanes = lax.broadcasted_iota(jnp.int32, (8, 128), 1)
        comb = jnp.zeros((8, 128), F32)
        for k in range(ids.shape[1]):
            comb = comb + jnp.where(lanes == ids[:, k : k + 1], wts[:, k : k + 1], 0.0)
        for r in (0, 1):
            cols = pl.ds(pl.multiple_of((2 * r + tp) * ds, 128), ds)
            scaled = (tok[0, :, cols].astype(F32) * inv * gain[:, cols]).astype(BF)
            if r == 0:
                xsend[:, :ds] = scaled
                xsend[:, ds:] = comb.astype(BF)
            else:
                xpair[x, :, :ds] = scaled
                xpair[x, :, ds:] = comb.astype(BF)

    pl.semaphore_wait(barrier, others)

    @pl.when(role == 1)
    def _():
        rcopy(xsend, xpair.at[x], snd.at[1], a0r.at[1], dev(0, z, 1 - x, y, tp)).start()
        rcopy(xpair.at[x], xpair.at[x], snd.at[2], a0r.at[1], dev(1, z, 1 - x, y, tp)).start()
        rcopy(xsend, xpair.at[x], snd.at[0], a0r.at[0], dev(0, z, x, y, tp)).start()

    def latent_send():
        for a in range(na):
            ts[a] = tok[0, :, a * fa : (a + 1) * fa]
        for d in range(1, na):
            ap = (a_me + d) % na
            rcopy(ts.at[ap], tr.at[a_me], snd.at[3], one.at[0], dev(role, ap // NX, ap % NX, y, tp)).start()
        for d in range(1, n):
            rcopy(kvw, wb.at[role, y], snd.at[4], one.at[1], dev(role, z, x, (y + d) % n, tp)).start()
        tr[a_me] = ts[a_me]
        wb[role, y] = kvw[...]

    def latent_swap():
        drain(wb.at[role, 0 : n - 1], one.at[1])
        rcopy(wb.at[role], wb.at[role], snd.at[5], one.at[2], dev(1 - role, z, x, y, tp)).start()

    def latent_project():
        drain(tr.at[0 : na - 1], one.at[0])
        drain(wb.at[0], one.at[2])
        rows = lax.broadcasted_iota(jnp.int32, (kc, 2 * kc), 0)
        cols = lax.broadcasted_iota(jnp.int32, (kc, 2 * kc), 1)
        weight = jnp.zeros((fa, 2 * kc), F32)
        for r in (0, 1):
            place = jnp.where(cols == rows + r * kc, 1.0, 0.0).astype(BF)
            block = wb[r].astype(F32).reshape(fa, kc).astype(BF)
            weight = weight + jnp.dot(block, place, preferred_element_type=F32)
        tokens = tr[...].astype(F32).reshape(na * 8, fa).astype(BF)
        share = jnp.dot(tokens, weight.astype(BF), preferred_element_type=F32)
        pk[...] = share.reshape(na, 8, 2 * kc)
        for d in range(1, na):
            ap = (a_me + d) % na
            rcopy(pk.at[ap], pkr.at[a_me], snd.at[6], one.at[3], dev(role, ap // NX, ap % NX, y, tp)).start()
        pkr[a_me] = pk[a_me]

    def latent_sum():
        drain(pkr.at[0 : na - 1], one.at[3])
        raw = jnp.sum(pkr[...], axis=0).astype(BF)

        @pl.when(role == 1)
        def _():
            rn[tp] = raw
            for k in (1, 2, 3):
                rcopy(
                    rn.at[tp], rn.at[tp], snd.at[7], k5n.at[tp], dev(peers[k][0], z, x, y, peers[k][1])
                ).start()

        @pl.when(role == 0)
        def _():
            ry[y] = raw
            for d in range(1, n):
                rcopy(ry.at[y], ry.at[y], snd.at[8], one.at[4], dev(role, z, x, (y + d) % n, tp)).start()

    def handoff_send():
        @pl.when(role == 0)
        def _():
            drain(ry.at[0 : n - 1], one.at[4])
            p_at = lax.broadcasted_iota(jnp.int32, (na * n, n * 8), 0)
            l_at = lax.broadcasted_iota(jnp.int32, (na * n, n * 8), 1)
            pick = jnp.where(p_at == a_me * n + l_at // 8, 1.0, 0.0).astype(BF)
            names = jnp.broadcast_to(part[...].astype(F32), (8, na * n)).astype(BF)
            dest = jnp.dot(names, pick, preferred_element_type=F32)[0:1]
            r_at = lax.broadcasted_iota(jnp.int32, (na * 8, n * 8), 0)
            c_at = lax.broadcasted_iota(jnp.int32, (na * 8, n * 8), 1)
            wanted = (r_at // 8 * n + y).astype(F32)
            move = jnp.where(
                jnp.logical_and(wanted == dest, r_at % 8 == c_at % 8), 1.0, 0.0
            ).astype(BF)
            held = ry[...].astype(F32).reshape(n * 8, 2 * kc).astype(BF)
            moved = jnp.dot(move, held, preferred_element_type=F32)
            rzs[...] = moved.reshape(na, 8, 2 * kc).astype(BF)
            for d in range(1, na):
                ap = (a_me + d) % na
                rcopy(rzs.at[ap], rz.at[a_me], snd.at[9], one.at[5], dev(role, ap // NX, ap % NX, y, tp)).start()
            rz[a_me] = rzs[a_me]

    def handoff_share():
        @pl.when(role == 0)
        def _():
            drain(rz.at[0 : na - 1], one.at[5])
            rp[tp] = jnp.sum(rz[...].astype(F32), axis=0).astype(BF)
            for k in (1, 2, 3):
                rcopy(
                    rp.at[tp], rp.at[tp], snd.at[10], k7r.at[tp], dev(peers[k][0], z, x, y, peers[k][1])
                ).start()

    def make_keys():
        for t in (0, 1):
            @pl.when(jnp.logical_not(jnp.logical_and(role == 1, tp == t)))
            def _():
                drain(rn.at[t], k5n.at[t])

            @pl.when(jnp.logical_not(jnp.logical_and(role == 0, tp == t)))
            def _():
                drain(rp.at[t], k7r.at[t])

        rows = lax.broadcasted_iota(jnp.int32, (2 * kc, 4 * kc), 0)
        cols = lax.broadcasted_iota(jnp.int32, (2 * kc, 4 * kc), 1)
        raw = jnp.zeros((16, 4 * kc), F32)
        for t in (0, 1):
            target = rows + t * kc + jnp.where(rows >= kc, kc, 0)
            place = jnp.where(cols == target, 1.0, 0.0).astype(BF)
            both = jnp.concatenate([rp[t].astype(F32), rn[t].astype(F32)], axis=0).astype(BF)
            raw = raw + jnp.dot(both, place, preferred_element_type=F32)
        latent = raw[:, :LATENT]
        inv = lax.rsqrt(jnp.mean(latent * latent, axis=1, keepdims=True) + EPSILON)
        rotary = raw[:, LATENT:]
        at0 = lax.broadcasted_iota(jnp.int32, (ROPE, ROPE), 0)
        at1 = lax.broadcasted_iota(jnp.int32, (ROPE, ROPE), 1)
        swap = jnp.where(at0 == at1 + 1 - 2 * (at1 % 2), 1.0, 0.0).astype(BF)
        swapped = jnp.dot(rotary.astype(BF), swap, preferred_element_type=F32)
        row = lax.broadcasted_iota(jnp.int32, (16, ROPE), 0)
        lane = lax.broadcasted_iota(jnp.int32, (16, ROPE), 1)
        position = jnp.where(row < 8, row + lens[0], 0)
        for b in range(8):
            position = position + jnp.where(row == 8 + b, lens[b] + (8 if b == 0 else 0), 0)
        frequency = jnp.exp((lane // 2).astype(F32) * (-2.0 / ROPE * math.log(10000.0)))
        angle = position.astype(F32) * frequency
        sign = jnp.where(lane % 2 == 0, -1.0, 1.0)
        turned = rotary * jnp.cos(angle) + swapped * sign * jnp.sin(angle)
        kx[:, :LATENT] = (latent * inv * kvg[...]).astype(BF)
        kx[:, LATENT:] = turned.astype(BF)

    def attend(b):
        count = cache_hbm.shape[1]
        kb[b, count : count + 16] = kx[...]
        score = lax.dot_general(
            qv[b], kb[b], (((1,), (1,)), ((), ())), preferred_element_type=F32
        ) * ((NOPE + ROPE) ** (-0.5))
        lane = lax.broadcasted_iota(jnp.int32, score.shape, 1)
        keep = jnp.logical_or(lane < lens[b], lane == count + 8 + b)
        if b == 0:
            keep = jnp.logical_or(keep, jnp.logical_and(lane >= count, lane < count + 8))
        score = jnp.where(keep, score, -jnp.inf)
        top = jnp.max(score, axis=1, keepdims=True)
        weight = jnp.exp(score - top)
        weight = (weight / jnp.sum(weight, axis=1, keepdims=True)).astype(BF)
        att[b] = jnp.dot(weight, kb[b, :, :LATENT], preferred_element_type=F32).astype(BF)

    h_me = (y + z) % 2
    j_me = jnp.where(h_me == 0, y // 2, z // 2)

    def neighbour(q):
        step = 1 - 2 * (q % 2)
        if q < 2:
            return dev(role, (z + step) % n, x, y, tp)
        return dev(role, z, x, (y + step) % n, tp)

    def gather_start():
        @pl.when(role == 0)
        def _():
            drain(xpair.at[0], a0r.at[0])

        drain(xpair.at[0], a0r.at[1])
        pair = jnp.concatenate([xpair[0].astype(F32), xpair[1].astype(F32)], axis=0)
        q_me, jj = 2 * h_me + j_me // cd, j_me % cd
        mine = xg.at[0, q_me, jj]
        mine[...] = pair.astype(BF)
        step = 1 - 2 * (j_me // cd)
        where = dev(role, (z + step * (1 - h_me)) % n, x, (y + step * h_me) % n, tp)
        rcopy(mine, xg.at[1, q_me, jj], snd.at[12], a2r.at[1, q_me, jj], where).start()
        for d in range(1, n):
            where = dev(role, (z + d * h_me) % n, x, (y + d * (1 - h_me)) % n, tp)
            rcopy(mine, mine, snd.at[11], a1r.at[q_me, jj], where).start()

    def gather_step(k):
        for jj in range(cd):
            for q in range(4):
                here = xg.at[k, q, jj]

                def forward():
                    drain(here, a2r.at[k, q, jj] if k else a1r.at[q, jj])
                    if k < n - 1:
                        rcopy(
                            here, xg.at[k + 1, q, jj], snd.at[12], a2r.at[k + 1, q, jj], neighbour(q)
                        ).start()

                if k:
                    forward()
                else:
                    j = (q % 2) * cd + jj
                    mine = jnp.logical_and(h_me == q // 2, j_me == j)
                    pl.when(jnp.logical_not(mine))(forward)

    step_rows = 4 * cd * 16
    quarter = cd * 16

    def project_step(k):
        if k == 0:
            load_gu.wait()
        rows = xg[k].reshape(step_rows, ds + 128)
        share = jnp.dot(rows[:, :ds], gu[...], preferred_element_type=F32)
        pf[k] = share
        ps[k] = share.astype(BF)
        for i in (1, 2, 3):
            there = pl.ds(pl.multiple_of((peers[i][0] * 2 + peers[i][1]) * quarter, quarter), quarter)
            rcopy(
                ps.at[k, there], pr.at[k, i - 1], snd.at[13], b1r.at[k, i - 1],
                dev(peers[i][0], z, x, y, peers[i][1]),
            ).start()

    def hidden_step(k):
        mine = pl.ds(pl.multiple_of(group * quarter, quarter), quarter)
        total = pf[k, mine]
        for i in (1, 2, 3):
            drain(pr.at[k, i - 1], b1r.at[k, i - 1])
            total = total + pr[k, i - 1].astype(F32)
        width = total.shape[1] // 2
        gate = total[:, :width]
        table = xg[k, group].reshape(quarter, ds + 128)[:, ds:].astype(F32)
        lanes = lax.broadcasted_iota(jnp.int32, (quarter, 128), 1)
        weight = jnp.sum(jnp.where(lanes == a_me, table, 0.0), axis=1, keepdims=True)
        hb[k, mine] = (gate / (1.0 + jnp.exp(-gate)) * total[:, width:] * weight).astype(BF)
        for i in (1, 2, 3):
            rcopy(
                hb.at[k, mine], hb.at[k, mine], snd.at[14], b2r.at[k, i - 1],
                dev(peers[i][0], z, x, y, peers[i][1]),
            ).start()

    def down_step(k):
        if k == 0:
            load_dn.wait()
        for i in (1, 2, 3):
            drain(hb.at[k, 0:quarter], b2r.at[k, i - 1])
        result = jnp.dot(hb[k], dn[...], preferred_element_type=F32)
        out[k] = result.astype(BF).reshape(4, cd, 16, ds)

    def sum_step(k):
        for jj in range(cd):
            for q in range(4):
                if k == 1:
                    here = out.at[k, q, jj]
                else:
                    here = cr.at[k - 2, q, jj]
                    drain(here, c2r.at[k - 2, q, jj])
                    here[...] = (here[...].astype(F32) + out[k, q, jj].astype(F32)).astype(BF)
                rcopy(
                    here, cr.at[k - 1, q, jj], snd.at[15], c2r.at[k - 1, q, jj], neighbour(q)
                ).start()

    def deliver():
        for jj in range(cd):
            for q in range(4):
                h, j = q // 2, (q % 2) * cd + jj
                here = cr.at[n - 2, q, jj]
                drain(here, c2r.at[n - 2, q, jj])
                total = out[0, q, jj].astype(F32) + here[...].astype(F32)
                if h == 0:
                    zz, yy, at = z, 2 * j + z % 2, y * NX + x
                else:
                    zz, yy, at = 2 * j + (1 - y % 2), y, z * NX + x
                for xd in (0, 1):
                    piece = fs.at[h, j, xd]
                    piece[...] = total[8 * xd : 8 * xd + 8].astype(BF)
                    itself = jnp.logical_and(jnp.logical_and(h_me == h, j_me == j), x == xd)

                    @pl.when(itself)
                    def _():
                        cf[at] = piece[...]

                    @pl.when(jnp.logical_not(itself))
                    def _():
                        rcopy(
                            piece, cf.at[at], snd.at[16], one.at[6], dev(role, zz, xd, yy, tp)
                        ).start()

    gather_start()
    latent_send()
    gather_step(0)
    project_step(0)
    latent_swap()
    for k in range(1, n):
        gather_step(k)
        project_step(k)
        hidden_step(k - 1)
        if k >= 2:
            down_step(k - 2)
        if k >= 3:
            sum_step(k - 2)
        if k == 1:
            latent_project()
        if k == 3:
            latent_sum()
        if k == 4:
            handoff_send()
        if k == 6:
            handoff_share()
    hidden_step(n - 1)
    down_step(n - 2)
    sum_step(n - 2)
    down_step(n - 1)
    sum_step(n - 1)
    load_q.wait()
    load_cache.wait()
    make_keys()
    for b in range(8):
        attend(b)
    deliver()
    drain(cf.at[0 : 2 * n - 1], one.at[6])
    moe_out[...] = jnp.sum(cf[...].astype(F32), axis=0).astype(BF)

    @pl.when(role == 1)
    def _():
        for i in (0, 1, 2):
            drain(xsend, snd.at[i])
        drain(rz.at[0:3], snd.at[7])

    @pl.when(role == 0)
    def _():
        drain(ry.at[0 : n - 1], snd.at[8])
        drain(rz.at[0 : na - 1], snd.at[9])
        drain(rz.at[0:3], snd.at[10])

    drain(tr.at[0 : na - 1], snd.at[3])
    drain(wb.at[0, 0 : n - 1], snd.at[4])
    drain(wb.at[0], snd.at[5])
    drain(pkr.at[0 : na - 1], snd.at[6])
    drain(xg.at[0 : n - 1, 0, 0], snd.at[11])
    drain(xg.at[0 : n - 1], snd.at[12])
    drain(pr, snd.at[13])
    drain(hb.at[:, 0 : 3 * quarter], snd.at[14])
    drain(cr, snd.at[15])
    drain(cf.at[0 : 2 * n - 1], snd.at[16])


def fused(n, tok, gain, ids, wts, part, kvg, lens, kvw, gu, dn, queries, cache):
    ch = n // 2
    cd = ch // 2
    step_rows = 4 * cd * 16
    _, ds, f2 = gu.shape
    dsx = ds + 128
    fe, kc = kvw.shape
    na = NX * n
    heads, width = queries.shape[1:]
    vm = pl.BlockSpec(memory_space=pltpu.VMEM)
    sm = pl.BlockSpec(memory_space=pltpu.SMEM)
    hbm = pl.BlockSpec(memory_space=pl.ANY)
    dma = pltpu.SemaphoreType.DMA
    scratch = [
        pltpu.VMEM((ds, f2), BF),
        pltpu.VMEM((f2 // 2, ds), BF),
        pltpu.VMEM((8, heads, width), BF),
        pltpu.VMEM((8, cache.shape[1] + 16, width), BF),
        pltpu.VMEM((8, dsx), BF),
        pltpu.VMEM((2, 8, dsx), BF),
        pltpu.VMEM((n, 4, cd, 16, dsx), BF),
        pltpu.VMEM((n, step_rows, f2), F32),
        pltpu.VMEM((n, step_rows, f2), BF),
        pltpu.VMEM((n, 3, step_rows // 4, f2), BF),
        pltpu.VMEM((n, step_rows, f2 // 2), BF),
        pltpu.VMEM((n, 4, cd, 16, ds), BF),
        pltpu.VMEM((n - 1, 4, cd, 16, ds), BF),
        pltpu.VMEM((2, ch, 2, 8, ds), BF),
        pltpu.VMEM((2 * n, 8, ds), BF),
        pltpu.VMEM((na, 8, n * fe), BF),
        pltpu.VMEM((na, 8, n * fe), BF),
        pltpu.VMEM((2, n, fe, kc), BF),
        pltpu.VMEM((na, 8, 2 * kc), F32),
        pltpu.VMEM((na, 8, 2 * kc), F32),
        pltpu.VMEM((2, 8, 2 * kc), BF),
        pltpu.VMEM((n, 8, 2 * kc), BF),
        pltpu.VMEM((na, 8, 2 * kc), BF),
        pltpu.VMEM((na, 8, 2 * kc), BF),
        pltpu.VMEM((2, 8, 2 * kc), BF),
        pltpu.VMEM((16, width), BF),
        dma((2,)),
        dma((4, cd)),
        dma((n, 4, cd)),
        dma((n, 3)),
        dma((n, 3)),
        dma((n - 1, 4, cd)),
        dma((2,)),
        dma((2,)),
        dma((7,)),
        dma((17,)),
        dma((4,)),
    ]
    return pl.pallas_call(
        functools.partial(fused_kernel, n),
        out_shape=(
            jax.ShapeDtypeStruct((8, heads, LATENT), BF),
            jax.ShapeDtypeStruct((8, ds), BF),
        ),
        in_specs=[vm] * 6 + [sm] + [vm] + [hbm] * 4,
        out_specs=(vm, vm),
        scratch_shapes=scratch,
        compiler_params=pltpu.CompilerParams(
            collective_id=0, has_side_effects=True, vmem_limit_bytes=56 * 1024 * 1024
        ),
    )(tok, gain, ids, wts, part, kvg, lens, kvw, gu, dn, queries, cache)


def per_device(
    n,
    pool_rows,
    kv_weight,
    kv_gain,
    latent_cache,
    queries,
    cache_lengths,
    partner,
    expert_ids,
    expert_weights,
    moe_gain,
    gate_up,
    down_proj,
):
    return fused(
        n,
        pool_rows,
        moe_gain[None, :],
        expert_ids,
        expert_weights,
        partner[None, :],
        kv_gain[None, :],
        cache_lengths,
        kv_weight,
        gate_up,
        down_proj,
        queries,
        latent_cache,
    )


def solution(mesh):
    n = round((mesh.shape["ep"] // NX) ** 0.5)
    in_specs = (
        P("role", "ep", None),
        P("ep", ("role", "tp")),
        P(),
        P("ep", None, None),
        P("ep", ("role", "tp"), None),
        P("ep"),
        P(),
        P("ep", None),
        P("ep", None),
        P(),
        P("ep", ("role", "tp"), None),
        P("ep", None, ("role", "tp")),
    )
    out_specs = (P("ep", ("role", "tp"), None), P("ep", ("role", "tp")))
    return jax.shard_map(
        functools.partial(per_device, n),
        mesh=mesh, in_specs=in_specs, out_specs=out_specs, check_vma=False,
    )
```

```python
import functools
import math

import jax
import jax.numpy as jnp
from jax import lax
from jax.experimental import pallas as pl
from jax.experimental.pallas import tpu as pltpu
from jax.sharding import PartitionSpec as P

MESH = pl.DeviceIdType.MESH
BF = jnp.bfloat16
F32 = jnp.float32
LATENT = 512
ROPE = 64
NOPE = 128
NX = 2
EPSILON = 1e-06


def fused_kernel(
    n, tok, gain, ids, wts, part, kvg, lens, kvw, gu_hbm, dn_hbm, q_hbm, cache_hbm,
    att, moe_out,
    gu, dn, qv, kb,
    xsend, xpair, xg, pf, ps, pr, hb, out, cr, fs, cf,
    ts, tr, wb, pk, pkr, rn, ry, rzs, rz, rp, kx,
    a0r, a1r, a2r, b1r, b2r, c2r, k5n, k7r, one, snd, loc, wr,
):
    role, ep, tp = lax.axis_index("role"), lax.axis_index("ep"), lax.axis_index("tp")
    z, x, y = ep // (NX * n), (ep // n) % NX, ep % n
    a_me = ep // n
    na = NX * n
    ch = n // 2
    ds = gu.shape[0]
    fe, kc = kvw.shape
    fa = n * fe
    group = role * 2 + tp

    def dev(r, zz, xx, yy, t):
        return (r, (zz * NX + xx) * n + yy, t)

    def rcopy(src, dst, s, r, device):
        return pltpu.make_async_remote_copy(
            src_ref=src, dst_ref=dst, send_sem=s, recv_sem=r, device_id=device, device_id_type=MESH
        )

    def drain(ref, sem):
        pltpu.make_async_copy(ref, ref, sem).wait()

    barrier = pltpu.get_barrier_semaphore()
    others = 0
    for xx in (0, 1):
        ox = (x + xx) % NX
        for d in range(n):
            if xx == 0 and d == 0:
                continue
            pl.semaphore_signal(
                barrier, inc=1, device_id=dev(role, z, ox, (y + d) % n, tp), device_id_type=MESH
            )
            others += 1
            if d:
                pl.semaphore_signal(
                    barrier, inc=1, device_id=dev(role, (z + d) % n, ox, y, tp), device_id_type=MESH
                )
                others += 1
    peers = [((role + (k >> 1)) % 2, (tp + (k & 1)) % 2) for k in range(4)]
    for k in (1, 2, 3):
        pl.semaphore_signal(
            barrier, inc=1, device_id=dev(peers[k][0], z, x, y, peers[k][1]), device_id_type=MESH
        )
        others += 1
    pl.semaphore_signal(
        barrier, inc=1, device_id=dev(1 - role, z, 1 - x, y, tp), device_id_type=MESH
    )
    others += 1

    load_gu = pltpu.make_async_copy(gu_hbm.at[0], gu, loc.at[0])
    load_dn = pltpu.make_async_copy(dn_hbm.at[0], dn, loc.at[1])
    load_q = pltpu.make_async_copy(q_hbm, qv, loc.at[2])
    load_cache = pltpu.make_async_copy(cache_hbm, kb.at[:, 0 : cache_hbm.shape[1]], loc.at[3])
    load_gu.start()
    load_dn.start()
    load_q.start()
    load_cache.start()

    @pl.when(role == 1)
    def _():
        xf = tok[0].astype(F32)
        inv = lax.rsqrt(jnp.mean(xf * xf, axis=1, keepdims=True) + EPSILON)
        lanes = lax.broadcasted_iota(jnp.int32, (8, 128), 1)
        comb = jnp.zeros((8, 128), F32)
        for k in range(ids.shape[1]):
            comb = comb + jnp.where(lanes == ids[:, k : k + 1], wts[:, k : k + 1], 0.0)
        for r in (0, 1):
            cols = pl.ds(pl.multiple_of((2 * r + tp) * ds, 128), ds)
            scaled = (tok[0, :, cols].astype(F32) * inv * gain[:, cols]).astype(BF)
            if r == 0:
                xsend[:, :ds] = scaled
                xsend[:, ds:] = comb.astype(BF)
            else:
                xpair[x, :, :ds] = scaled
                xpair[x, :, ds:] = comb.astype(BF)

    for a in range(na):
        ts[a] = tok[0, :, a * fa : (a + 1) * fa]

    pl.semaphore_wait(barrier, others)

    @pl.when(role == 1)
    def _():
        rcopy(xsend, xpair.at[x], snd.at[1], a0r.at[1], dev(0, z, 1 - x, y, tp)).start()
        rcopy(xpair.at[x], xpair.at[x], snd.at[2], a0r.at[1], dev(1, z, 1 - x, y, tp)).start()
        rcopy(xsend, xpair.at[x], snd.at[0], a0r.at[0], dev(0, z, x, y, tp)).start()

    def latent_send():
        for d in range(1, na):
            ap = (a_me + d) % na
            rcopy(ts.at[ap], tr.at[a_me], snd.at[3], one.at[0], dev(role, ap // NX, ap % NX, y, tp)).start()
        for d in range(1, n):
            rcopy(kvw, wb.at[role, y], snd.at[4], one.at[1], dev(role, z, x, (y + d) % n, tp)).start()
        tr[a_me] = ts[a_me]
        wb[role, y] = kvw[...]

    def latent_swap():
        drain(wb.at[role, 0 : n - 1], one.at[1])
        rcopy(wb.at[role], wb.at[role], snd.at[5], one.at[2], dev(1 - role, z, x, y, tp)).start()

    def latent_project():
        drain(tr.at[0 : na - 1], one.at[0])
        drain(wb.at[0], one.at[2])
        rows = lax.broadcasted_iota(jnp.int32, (kc, 2 * kc), 0)
        cols = lax.broadcasted_iota(jnp.int32, (kc, 2 * kc), 1)
        weight = jnp.zeros((fa, 2 * kc), F32)
        for r in (0, 1):
            place = jnp.where(cols == rows + r * kc, 1.0, 0.0).astype(BF)
            block = wb[r].astype(F32).reshape(fa, kc).astype(BF)
            weight = weight + jnp.dot(block, place, preferred_element_type=F32)
        tokens = tr[...].astype(F32).reshape(na * 8, fa).astype(BF)
        share = jnp.dot(tokens, weight.astype(BF), preferred_element_type=F32)
        pk[...] = share.reshape(na, 8, 2 * kc).astype(BF)
        for d in range(1, na):
            ap = (a_me + d) % na
            rcopy(pk.at[ap], pkr.at[a_me], snd.at[6], one.at[3], dev(role, ap // NX, ap % NX, y, tp)).start()
        pkr[a_me] = pk[a_me]

    def latent_sum():
        drain(pkr.at[0 : na - 1], one.at[3])
        raw = jnp.sum(pkr[...].astype(F32), axis=0).astype(BF)

        @pl.when(role == 1)
        def _():
            rn[tp] = raw
            for k in (1, 2, 3):
                rcopy(
                    rn.at[tp], rn.at[tp], snd.at[7], k5n.at[tp], dev(peers[k][0], z, x, y, peers[k][1])
                ).start()

        @pl.when(role == 0)
        def _():
            ry[y] = raw
            for d in range(1, n):
                rcopy(ry.at[y], ry.at[y], snd.at[8], one.at[4], dev(role, z, x, (y + d) % n, tp)).start()

    def handoff_send():
        @pl.when(role == 0)
        def _():
            drain(ry.at[0 : n - 1], one.at[4])
            p_at = lax.broadcasted_iota(jnp.int32, (na * n, n * 8), 0)
            l_at = lax.broadcasted_iota(jnp.int32, (na * n, n * 8), 1)
            pick = jnp.where(p_at == a_me * n + l_at // 8, 1.0, 0.0).astype(BF)
            names = jnp.broadcast_to(part[...].astype(F32), (8, na * n)).astype(BF)
            dest = jnp.dot(names, pick, preferred_element_type=F32)[0:1]
            r_at = lax.broadcasted_iota(jnp.int32, (na * 8, n * 8), 0)
            c_at = lax.broadcasted_iota(jnp.int32, (na * 8, n * 8), 1)
            wanted = (r_at // 8 * n + y).astype(F32)
            move = jnp.where(
                jnp.logical_and(wanted == dest, r_at % 8 == c_at % 8), 1.0, 0.0
            ).astype(BF)
            held = ry[...].astype(F32).reshape(n * 8, 2 * kc).astype(BF)
            moved = jnp.dot(move, held, preferred_element_type=F32)
            rzs[...] = moved.reshape(na, 8, 2 * kc).astype(BF)
            for d in range(1, na):
                ap = (a_me + d) % na
                rcopy(rzs.at[ap], rz.at[a_me], snd.at[9], one.at[5], dev(role, ap // NX, ap % NX, y, tp)).start()
            rz[a_me] = rzs[a_me]

    def handoff_share():
        @pl.when(role == 0)
        def _():
            drain(rz.at[0 : na - 1], one.at[5])
            rp[tp] = jnp.sum(rz[...].astype(F32), axis=0).astype(BF)
            for k in (1, 2, 3):
                rcopy(
                    rp.at[tp], rp.at[tp], snd.at[10], k7r.at[tp], dev(peers[k][0], z, x, y, peers[k][1])
                ).start()

    def make_keys():
        for t in (0, 1):
            @pl.when(jnp.logical_not(jnp.logical_and(role == 1, tp == t)))
            def _():
                drain(rn.at[t], k5n.at[t])

            @pl.when(jnp.logical_not(jnp.logical_and(role == 0, tp == t)))
            def _():
                drain(rp.at[t], k7r.at[t])

        rows = lax.broadcasted_iota(jnp.int32, (2 * kc, 4 * kc), 0)
        cols = lax.broadcasted_iota(jnp.int32, (2 * kc, 4 * kc), 1)
        raw = jnp.zeros((16, 4 * kc), F32)
        for t in (0, 1):
            target = rows + t * kc + jnp.where(rows >= kc, kc, 0)
            place = jnp.where(cols == target, 1.0, 0.0).astype(BF)
            both = jnp.concatenate([rp[t].astype(F32), rn[t].astype(F32)], axis=0).astype(BF)
            raw = raw + jnp.dot(both, place, preferred_element_type=F32)
        latent = raw[:, :LATENT]
        inv = lax.rsqrt(jnp.mean(latent * latent, axis=1, keepdims=True) + EPSILON)
        rotary = raw[:, LATENT:]
        at0 = lax.broadcasted_iota(jnp.int32, (ROPE, ROPE), 0)
        at1 = lax.broadcasted_iota(jnp.int32, (ROPE, ROPE), 1)
        swap = jnp.where(at0 == at1 + 1 - 2 * (at1 % 2), 1.0, 0.0).astype(BF)
        swapped = jnp.dot(rotary.astype(BF), swap, preferred_element_type=F32)
        row = lax.broadcasted_iota(jnp.int32, (16, ROPE), 0)
        lane = lax.broadcasted_iota(jnp.int32, (16, ROPE), 1)
        position = jnp.where(row < 8, row + lens[0], 0)
        for b in range(8):
            position = position + jnp.where(row == 8 + b, lens[b] + (8 if b == 0 else 0), 0)
        frequency = jnp.exp((lane // 2).astype(F32) * (-2.0 / ROPE * math.log(10000.0)))
        angle = position.astype(F32) * frequency
        sign = jnp.where(lane % 2 == 0, -1.0, 1.0)
        turned = rotary * jnp.cos(angle) + swapped * sign * jnp.sin(angle)
        kx[:, :LATENT] = (latent * inv * kvg[...]).astype(BF)
        kx[:, LATENT:] = turned.astype(BF)

    def attend(b):
        count = cache_hbm.shape[1]
        kb[b, count : count + 16] = kx[...]
        score = lax.dot_general(
            qv[b], kb[b], (((1,), (1,)), ((), ())), preferred_element_type=F32
        ) * ((NOPE + ROPE) ** (-0.5))
        lane = lax.broadcasted_iota(jnp.int32, score.shape, 1)
        keep = jnp.logical_or(lane < lens[b], lane == count + 8 + b)
        if b == 0:
            keep = jnp.logical_or(keep, jnp.logical_and(lane >= count, lane < count + 8))
        score = jnp.where(keep, score, -jnp.inf)
        top = jnp.max(score, axis=1, keepdims=True)
        weight = jnp.exp(score - top)
        weight = (weight / jnp.sum(weight, axis=1, keepdims=True)).astype(BF)
        att[b] = jnp.dot(weight, kb[b, :, :LATENT], preferred_element_type=F32).astype(BF)

    h_me = (y + z) % 2
    line = jnp.where(h_me == 0, y, z)

    def neighbour(q):
        step = 1 - 2 * (q % 2)
        if q < 2:
            return dev(role, (z + step) % n, x, y, tp)
        return dev(role, z, x, (y + step) % n, tp)

    def gather_start():
        @pl.when(role == 0)
        def _():
            drain(xpair.at[0], a0r.at[0])

        drain(xpair.at[0], a0r.at[1])
        pair = jnp.concatenate([xpair[0].astype(F32), xpair[1].astype(F32)], axis=0)
        mine = xg.at[0, 0, 2 * h_me]
        mine[...] = pair.astype(BF)
        where = dev(role, (z + 1 - h_me) % n, x, (y + h_me) % n, tp)
        rcopy(mine, xg.at[1, 0, 2 * h_me], snd.at[12], a2r.at[1, 0, 2 * h_me], where).start()
        for d in (1, n - 1, 2, n - 2, 3, n - 3, 4):
            where = dev(role, (z + d * h_me) % n, x, (y + d * (1 - h_me)) % n, tp)
            e = ((line + d) % n // 2 - line // 2 + ch) % ch
            w, q = e // 2, 2 * h_me + e % 2
            rcopy(mine, xg.at[0, w, q], snd.at[11], a1r.at[w, q], where).start()

    def gather_step(k, w):
        for q in range(4):
            here = xg.at[k, w, q]

            def forward():
                drain(here, a2r.at[k, w, q] if k else a1r.at[w, q])
                if k < n - 1:
                    rcopy(
                        here, xg.at[k + 1, w, q], snd.at[12], a2r.at[k + 1, w, q], neighbour(q)
                    ).start()

            if k == 0 and w == 0 and q % 2 == 0:
                pl.when(h_me != q // 2)(forward)
            else:
                forward()

    def project_step(k, w):
        if k == 0 and w == 0:
            load_gu.wait()
        rows = xg[k, w].reshape(64, ds + 128)
        share = jnp.dot(rows[:, :ds], gu[...], preferred_element_type=F32)
        pf[k, w] = share
        ps[k, w] = share.astype(BF)
        for i in (1, 2, 3):
            there = pl.ds(pl.multiple_of((peers[i][0] * 2 + peers[i][1]) * 16, 16), 16)
            rcopy(
                ps.at[k, w, there], pr.at[k, w, i - 1], snd.at[13], b1r.at[k, w, i - 1],
                dev(peers[i][0], z, x, y, peers[i][1]),
            ).start()

    def hidden_step(k, w):
        mine = pl.ds(pl.multiple_of(group * 16, 16), 16)
        total = pf[k, w, mine]
        for i in (1, 2, 3):
            drain(pr.at[k, w, i - 1], b1r.at[k, w, i - 1])
            total = total + pr[k, w, i - 1].astype(F32)
        width = total.shape[1] // 2
        gate = total[:, :width]
        table = xg[k, w, group][:, ds:].astype(F32)
        lanes = lax.broadcasted_iota(jnp.int32, (16, 128), 1)
        weight = jnp.sum(jnp.where(lanes == a_me, table, 0.0), axis=1, keepdims=True)
        hb[k, w, mine] = (gate / (1.0 + jnp.exp(-gate)) * total[:, width:] * weight).astype(BF)
        for i in (1, 2, 3):
            rcopy(
                hb.at[k, w, mine], hb.at[k, w, mine], snd.at[14], b2r.at[k, w, i - 1],
                dev(peers[i][0], z, x, y, peers[i][1]),
            ).start()

    def down_step(k, w):
        if k == 0 and w == 0:
            load_dn.wait()
        for i in (1, 2, 3):
            drain(hb.at[k, w, 0:16], b2r.at[k, w, i - 1])
        result = jnp.dot(hb[k, w], dn[...], preferred_element_type=F32)
        out[k, w] = result.astype(BF).reshape(4, 16, ds)

    def sum_step(k, w):
        for q in range(4):
            if k == 1:
                here = out.at[k, w, q]
            else:
                here = cr.at[k - 2, w, q]
                drain(here, c2r.at[k - 2, w, q])
                here[...] = (here[...].astype(F32) + out[k, w, q].astype(F32)).astype(BF)
            rcopy(
                here, cr.at[k - 1, w, q], snd.at[15], c2r.at[k - 1, w, q], neighbour(q)
            ).start()

    def deliver(w):
        for q in range(4):
            h, e = q // 2, 2 * w + q % 2
            here = cr.at[n - 2, w, q]
            drain(here, c2r.at[n - 2, w, q])
            total = out[0, w, q].astype(F32) + here[...].astype(F32)
            if h == 0:
                zz, yy, at = z, (y // 2 - e + ch) % ch * 2 + z % 2, y * NX + x
            else:
                zz, yy, at = (z // 2 - e + ch) % ch * 2 + 1 - y % 2, y, z * NX + x
            for xd in (0, 1):
                piece = fs.at[w, q, xd]
                piece[...] = total[8 * xd : 8 * xd + 8].astype(BF)

                def send():
                    rcopy(piece, cf.at[at], snd.at[16], one.at[6], dev(role, zz, xd, yy, tp)).start()

                if e:
                    send()
                    continue
                itself = jnp.logical_and(h_me == h, x == xd)
                pl.when(jnp.logical_not(itself))(send)

                @pl.when(itself)
                def _():
                    cf[at] = piece[...]

    latent_send()
    gather_start()
    for u in range(2 * n + 4):
        if u < 2 * n:
            gather_step(u // 2, u % 2)
            project_step(u // 2, u % 2)
        if 0 <= u - 2 < 2 * n:
            hidden_step((u - 2) // 2, (u - 2) % 2)
        if u >= 4:
            down_step((u - 4) // 2, (u - 4) % 2)
        if u >= 6:
            sum_step((u - 4) // 2, (u - 4) % 2)
        if u == 4:
            latent_swap()
        if u == 7:
            latent_project()
        if u == 10:
            latent_sum()
        if u == 13:
            handoff_send()
        if u == 16:
            handoff_share()
    deliver(0)
    deliver(1)
    load_q.wait()
    load_cache.wait()
    make_keys()
    for b in range(8):
        attend(b)
    drain(cf.at[0 : 2 * n - 1], one.at[6])
    moe_out[...] = jnp.sum(cf[...].astype(F32), axis=0).astype(BF)

    @pl.when(role == 1)
    def _():
        for i in (0, 1, 2):
            drain(xsend, snd.at[i])
        drain(rz.at[0:3], snd.at[7])

    @pl.when(role == 0)
    def _():
        drain(ry.at[0 : n - 1], snd.at[8])
        drain(rz.at[0 : na - 1], snd.at[9])
        drain(rz.at[0:3], snd.at[10])

    drain(tr.at[0 : na - 1], snd.at[3])
    drain(wb.at[0, 0 : n - 1], snd.at[4])
    drain(wb.at[0], snd.at[5])
    drain(pkr.at[0 : na - 1], snd.at[6])
    drain(xg.at[0 : n - 1, 0, 0], snd.at[11])
    drain(xg.at[0 : n - 1], snd.at[12])
    drain(pr, snd.at[13])
    drain(hb.at[:, :, 0:48], snd.at[14])
    drain(cr, snd.at[15])
    drain(cf.at[0 : 2 * n - 1], snd.at[16])


def fused(n, tok, gain, ids, wts, part, kvg, lens, kvw, gu, dn, queries, cache):
    _, ds, f2 = gu.shape
    dsx = ds + 128
    fe, kc = kvw.shape
    na = NX * n
    heads, width = queries.shape[1:]
    vm = pl.BlockSpec(memory_space=pltpu.VMEM)
    sm = pl.BlockSpec(memory_space=pltpu.SMEM)
    hbm = pl.BlockSpec(memory_space=pl.ANY)
    dma = pltpu.SemaphoreType.DMA
    scratch = [
        pltpu.VMEM((ds, f2), BF),
        pltpu.VMEM((f2 // 2, ds), BF),
        pltpu.VMEM((8, heads, width), BF),
        pltpu.VMEM((8, cache.shape[1] + 16, width), BF),
        pltpu.VMEM((8, dsx), BF),
        pltpu.VMEM((2, 8, dsx), BF),
        pltpu.VMEM((n, 2, 4, 16, dsx), BF),
        pltpu.VMEM((n, 2, 64, f2), F32),
        pltpu.VMEM((n, 2, 64, f2), BF),
        pltpu.VMEM((n, 2, 3, 16, f2), BF),
        pltpu.VMEM((n, 2, 64, f2 // 2), BF),
        pltpu.VMEM((n, 2, 4, 16, ds), BF),
        pltpu.VMEM((n - 1, 2, 4, 16, ds), BF),
        pltpu.VMEM((2, 4, 2, 8, ds), BF),
        pltpu.VMEM((2 * n, 8, ds), BF),
        pltpu.VMEM((na, 8, n * fe), BF),
        pltpu.VMEM((na, 8, n * fe), BF),
        pltpu.VMEM((2, n, fe, kc), BF),
        pltpu.VMEM((na, 8, 2 * kc), BF),
        pltpu.VMEM((na, 8, 2 * kc), BF),
        pltpu.VMEM((2, 8, 2 * kc), BF),
        pltpu.VMEM((n, 8, 2 * kc), BF),
        pltpu.VMEM((na, 8, 2 * kc), BF),
        pltpu.VMEM((na, 8, 2 * kc), BF),
        pltpu.VMEM((2, 8, 2 * kc), BF),
        pltpu.VMEM((16, width), BF),
        dma((2,)),
        dma((2, 4)),
        dma((n, 2, 4)),
        dma((n, 2, 3)),
        dma((n, 2, 3)),
        dma((n - 1, 2, 4)),
        dma((2,)),
        dma((2,)),
        dma((7,)),
        dma((17,)),
        dma((4,)),
        dma((2, n // 2 + 1)),
    ]
    return pl.pallas_call(
        functools.partial(fused_kernel, n),
        out_shape=(
            jax.ShapeDtypeStruct((8, heads, LATENT), BF),
            jax.ShapeDtypeStruct((8, ds), BF),
        ),
        in_specs=[vm] * 6 + [sm] + [vm] + [hbm] * 4,
        out_specs=(vm, vm),
        scratch_shapes=scratch,
        compiler_params=pltpu.CompilerParams(
            collective_id=0, has_side_effects=True, vmem_limit_bytes=56 * 1024 * 1024
        ),
    )(tok, gain, ids, wts, part, kvg, lens, kvw, gu, dn, queries, cache)


def per_device(
    n,
    pool_rows,
    kv_weight,
    kv_gain,
    latent_cache,
    queries,
    cache_lengths,
    partner,
    expert_ids,
    expert_weights,
    moe_gain,
    gate_up,
    down_proj,
):
    return fused(
        n,
        pool_rows,
        moe_gain[None, :],
        expert_ids,
        expert_weights,
        partner[None, :],
        kv_gain[None, :],
        cache_lengths,
        kv_weight,
        gate_up,
        down_proj,
        queries,
        latent_cache,
    )


def solution(mesh):
    n = round((mesh.shape["ep"] // NX) ** 0.5)
    in_specs = (
        P("role", "ep", None),
        P("ep", ("role", "tp")),
        P(),
        P("ep", None, None),
        P("ep", ("role", "tp"), None),
        P("ep"),
        P(),
        P("ep", None),
        P("ep", None),
        P(),
        P("ep", ("role", "tp"), None),
        P("ep", None, ("role", "tp")),
    )
    out_specs = (P("ep", ("role", "tp"), None), P("ep", ("role", "tp")))
    return jax.shard_map(
        functools.partial(per_device, n),
        mesh=mesh, in_specs=in_specs, out_specs=out_specs, check_vma=False,
    )
```
